32 devices in a mesh: bus: 8 (over z, y), line: 4 (over x, core).
Axes of the slice: x: 2, y: 2, z: 4, core: 2. Of those that a mesh axis runs over, the one named last changes fastest.
Arguments:
- generation: bfloat16 [512, 16384], P(None, 'bus'), may hold values from -6 to 6
- profiles: float32 [24, 16384], P(None, 'bus'), may hold values from -5 to 5
- scen_profile: int32 [512], replicated, may hold values from 0 to 23
- ptdf: bfloat16 [16384, 16384], P('line', 'bus'), may hold values from -0.046875 to 0.046875
- lodf: float32 [1536, 512], P('line'), may hold values from -1 to 1
- limits: float32 [1536], P('line'), may hold values from 0.5 to 2
- monitored: int32 [1536], P('line'), may hold values from 0 to 16383, as said below
- outages: int32 [512], replicated, may hold values from 0 to 16383, as said below
- cost_quad: float32 [16384], P('bus'), may hold values from 0.5 to 2
Outputs:
- gradient: bfloat16 [512, 16384], P('line', 'bus')
- outage_flow: float32 [512, 512], P('bus')
- outage_sens: float32 [512, 512], P('bus')
The draws below stay inside these ranges and needn't reach their ends.
Inputs may be any that keep to these rules, and one draw needn't show every extreme that they name: `monitored`: the entries with positions k * 384 to (k + 1) * 384 - 1 are distinct line ids of the k-th block of 4096 lines (ids k * 4096 to (k + 1) * 4096 - 1). `outages`: distinct line ids; how many fall in each block of 4096 lines varies from block to block.
All inputs are finite; a program needn't handle non-finite values.
Results may differ from the reference program's by a relative error of at most 0.0029.
Values may be sent and summed in bfloat16 or wider, within the bound.
A program may use at most 64 MiB of HBM per device.

```python
import math
import jax
import jax.numpy as jnp
from jax import lax

LINES = 16384
BUSES = 16384
OUTAGES = 512
PROFILES = 24
MON_DEV = 384
SCEN = 512
MONITORED = 1536
N_BUS = 8
N_LINE = 4


def draw_monitored(key, part):
    line_rows = LINES // N_LINE

    def one_block(group):
        order = jax.random.permutation(jax.random.fold_in(key, group), line_rows)
        return order[:MON_DEV].astype(jnp.int32) + group * line_rows
    return jax.vmap(one_block)(jnp.arange(N_LINE, dtype=jnp.int32)).reshape(-1)


def draw_outages(key, part):
    line_rows = LINES // N_LINE
    tilted = jax.random.randint(jax.random.fold_in(key, 11), (N_LINE,), 0, 4)
    ranking = jax.random.permutation(jax.random.fold_in(key, 12), LINES).astype(jnp.int32)
    line_ids = jnp.arange(LINES, dtype=jnp.int32)
    scores = (ranking + tilted[line_ids // line_rows] * (LINES // 64)) * LINES + line_ids
    chosen = lax.top_k(scores, OUTAGES)[1]
    return chosen.astype(jnp.int32)


def with_ends(values, rng, least, largest):
    extent = values.shape
    spot = [jax.random.randint(jax.random.fold_in(rng, axis), (), 0, extent[axis]) for axis in range(len(extent))]
    values = values.at[tuple(spot)].set(least)
    longest = extent.index(max(extent))
    spot[longest] = (spot[longest] + 1) % extent[longest]
    return values.at[tuple(spot)].set(largest)


def block_levels(own_key, shape, split, least, largest):
    def one(position, blocks):
        heights = jax.random.uniform(jax.random.fold_in(jax.random.fold_in(own_key, 6), position), (blocks,), jnp.float32, least / len(split), largest / len(split))
        return jnp.repeat(jnp.exp(heights), shape[position] // blocks).reshape((-1,) + (1,) * (len(shape) - position - 1))

    loudness = one(*split[0])
    for cut in split[1:]:
        loudness = loudness * one(*cut)
    return loudness


def normal_values(rng, shape, spread, limit, cuts=(), held_as=jnp.bfloat16):
    loudness = block_levels(rng, shape, cuts, -0.22, 0.18) if cuts else 1.0
    result = jax.random.normal(rng, shape, jnp.float32) * spread * loudness
    return jnp.minimum(jnp.maximum(result, -limit), limit).astype(held_as)


def setup_inputs(seed: int = 0) -> dict:
    keys = jax.random.split(jax.random.key(seed), 10)
    generation = normal_values(keys[0], (SCEN, BUSES), 1.0, 6.0, ((1, 8),))
    profiles = normal_values(keys[1], (PROFILES, BUSES), 0.7, 5.0, ((1, 8),), jnp.float32)
    scen_profile = with_ends(jax.random.randint(keys[2], (SCEN,), 0, PROFILES), jax.random.fold_in(keys[2], 1), 0, PROFILES - 1).astype(jnp.int32)
    ptdf = normal_values(keys[3], (LINES, BUSES), BUSES ** -0.5, 0.046875, ((0, 4), (1, 8)))
    lodf = jnp.clip(jax.random.uniform(keys[4], (MONITORED, OUTAGES), jnp.float32, -1.0, 1.0) * block_levels(keys[4], (MONITORED, OUTAGES), ((0, 4),), -0.4, 0.0), -1.0, 1.0)
    limits = jnp.clip(jnp.exp(math.log(2.0) - 1.3862944 * jax.random.uniform(keys[5], (MONITORED,), jnp.float32) ** block_levels(keys[5], (MONITORED,), ((0, 4),), -0.2, 0.2)), 0.5, 2.0)
    monitored = draw_monitored(jax.random.fold_in(keys[9], 71), 0)
    outages = draw_outages(jax.random.fold_in(keys[9], 71), 0)
    cost_quad = jnp.clip(jnp.exp(math.log(2.0) - 1.3862944 * jax.random.uniform(keys[8], (BUSES,), jnp.float32) ** block_levels(keys[8], (BUSES,), ((0, 8),), -0.2, 0.2)), 0.5, 2.0)
    return dict(generation=generation, profiles=profiles, scen_profile=scen_profile, ptdf=ptdf, lodf=lodf, limits=limits, monitored=monitored, outages=outages, cost_quad=cost_quad)


sharpness = 4.0

def contingency(pieces, lodf, limits):
    base_block, outage_block = pieces
    post_flow = base_block[:, :, None] + lodf[None, :, :] * outage_block[:, None, :]
    bounds = limits[None, :, None]
    raw_slope = jax.nn.sigmoid(sharpness * (post_flow - bounds)) - jax.nn.sigmoid(sharpness * (-post_flow - bounds))
    direct = lax.optimization_barrier(jnp.sum(raw_slope, axis=2)) / OUTAGES
    sens_total = jnp.einsum('smk,mk->sk', raw_slope, lodf, precision=lax.Precision.HIGHEST)
    return (direct, sens_total)

def reference(generation, profiles, scen_profile, ptdf, lodf, limits, monitored, outages, cost_quad):
    injection = (generation.astype(jnp.float32) - profiles[scen_profile]).astype(jnp.bfloat16)
    bus_width = BUSES // N_BUS
    line_width = LINES // N_LINE

    def flow_group(group, running):
        columns = lax.dynamic_slice_in_dim(ptdf, group * bus_width, bus_width, 1).astype(jnp.float32)
        inputs = lax.dynamic_slice_in_dim(injection, group * bus_width, bus_width, 1).astype(jnp.float32)
        return running + jnp.dot(inputs, columns.T, precision=lax.Precision.HIGHEST)
    flows = lax.fori_loop(0, N_BUS, flow_group, jnp.zeros((SCEN, LINES), jnp.float32))
    base = flows[:, monitored]
    outflow = flows[:, outages]
    block_size = math.gcd(SCEN, 4)
    base_blocks = base.reshape(SCEN // block_size, block_size, MONITORED)
    outage_blocks = outflow.reshape(SCEN // block_size, block_size, OUTAGES)
    direct, sens_total = lax.map(lambda pieces: contingency(pieces, lodf, limits), (base_blocks, outage_blocks))
    direct = direct.reshape(SCEN, MONITORED)
    sens_total = sens_total.reshape(SCEN, OUTAGES)
    backward = sens_total / OUTAGES
    outage_sens = sens_total / math.sqrt(MONITORED)
    adjoint = jnp.zeros((SCEN, LINES), jnp.float32).at[:, monitored].add(direct)
    adjoint = adjoint.at[:, outages].add(backward).astype(jnp.bfloat16)

    def grad_group(group, running):
        row_block = lax.dynamic_slice_in_dim(ptdf, group * line_width, line_width, 0).astype(jnp.float32)
        inputs = lax.dynamic_slice_in_dim(adjoint, group * line_width, line_width, 1).astype(jnp.float32)
        return running + jnp.dot(inputs, row_block, precision=lax.Precision.HIGHEST)
    pushed = lax.fori_loop(0, N_LINE, grad_group, jnp.zeros((SCEN, BUSES), jnp.float32))
    gradient = (cost_quad[None, :] * generation.astype(jnp.float32) + pushed).astype(jnp.bfloat16)
    return (gradient, outflow, outage_sens)
```

```python
import functools
import math

import jax
import jax.numpy as jnp
from jax import lax
from jax.experimental import pallas as pl
from jax.experimental.pallas import tpu as pltpu
from jax.sharding import PartitionSpec as P

MESH = pl.DeviceIdType.MESH
HIGH = lax.Precision.HIGHEST
ROWS_DOT = (((1,), (1,)), ((), ()))
LANES = 128


def remote(src, dst, send_sem, recv_sem, axis, peer):
    return pltpu.make_async_remote_copy(
        src_ref=src,
        dst_ref=dst,
        send_sem=send_sem,
        recv_sem=recv_sem,
        device_id={axis: peer},
        device_id_type=MESH,
    )


def step_kernel(
    n_bus,
    n_line,
    inj_ref,
    rows_ref,
    lodf_ref,
    limits_ref,
    monitored_ref,
    outages_ref,
    keep_ref,
    generation_ref,
    cost_ref,
    gradient_ref,
    outflow_ref,
    sens_ref,
    out_part,
    out_got,
    out_sum,
    mon_part,
    mon_got,
    outbus_got,
    out_all,
    base_t,
    limit_wide,
    direct_t,
    flow2,
    sens_tall,
    sens_part,
    sens_got,
    adjoint,
    core_part,
    core_got,
    own_part,
    hi_send,
    hi_got,
    line_send,
    line_recv,
    mon_send,
    mon_recv,
    ob_send,
    ob_recv,
    oa_send,
    oa_recv,
    se_send,
    se_recv,
    ad_send,
    ad_recv,
    co_send,
    co_recv,
    hi_ssem,
    hi_rsem,
):
    scen, buses = inj_ref.shape
    count_m, count_k = lodf_ref.shape
    own = scen // n_bus
    width = count_k // n_line
    grad_rows = scen // n_line
    n_hi = n_line // 2
    b = lax.axis_index("bus")
    l = lax.axis_index("line")

    barrier = pltpu.get_barrier_semaphore()
    for d in range(1, n_bus):
        pl.semaphore_signal(
            barrier, inc=1, device_id={"bus": lax.rem(b + d, n_bus)}, device_id_type=MESH
        )
    for d in range(1, n_line):
        pl.semaphore_signal(
            barrier, inc=1, device_id={"line": lax.rem(l + d, n_line)}, device_id_type=MESH
        )
    for j in range(n_line):
        out_part[j] = lax.dot_general(
            inj_ref[...],
            rows_ref[count_m + j * width : count_m + (j + 1) * width, :],
            ROWS_DOT,
            preferred_element_type=jnp.float32,
        )
    pl.semaphore_wait(barrier, n_bus + n_line - 2)
    line_copies = []
    for d in range(1, n_line):
        peer = lax.rem(l + d, n_line)
        copy = remote(
            out_part.at[peer], out_got.at[d - 1], line_send.at[d - 1], line_recv.at[d - 1], "line", peer
        )
        copy.start()
        line_copies.append(copy)
    mon_part[...] = lax.dot_general(
        inj_ref[...], rows_ref[:count_m, :], ROWS_DOT, preferred_element_type=jnp.float32
    )
    mon_copies = []
    for d in range(1, n_bus):
        peer = lax.rem(b + d, n_bus)
        copy = remote(
            mon_part.at[pl.ds(pl.multiple_of(peer * own, own), own), :],
            mon_got.at[d - 1],
            mon_send.at[d - 1],
            mon_recv.at[d - 1],
            "bus",
            peer,
        )
        copy.start()
        mon_copies.append(copy)
    limit_wide[...] = jnp.broadcast_to(2.0 * limits_ref[...], limit_wide.shape)
    for copy in line_copies:
        copy.wait()
    total = out_part[l]
    for d in range(1, n_line):
        total = total + out_got[d - 1]
    out_sum[...] = total
    ob_copies = []
    for d in range(1, n_bus):
        peer = lax.rem(b + d, n_bus)
        copy = remote(
            out_sum.at[pl.ds(pl.multiple_of(peer * own, own), own), :],
            outbus_got.at[d - 1],
            ob_send.at[d - 1],
            ob_recv.at[d - 1],
            "bus",
            peer,
        )
        copy.start()
        ob_copies.append(copy)
    own_rows = pl.ds(pl.multiple_of(b * own, own), own)
    for copy in mon_copies:
        copy.wait()
    base = mon_part[own_rows, :]
    for d in range(1, n_bus):
        base = base + mon_got[d - 1]
    spread = jnp.concatenate([2.0 * base, jnp.zeros((LANES - own, count_m), jnp.float32)], axis=0)
    base_t[...] = spread.T
    for copy in ob_copies:
        copy.wait()
    flow = out_sum[own_rows, :]
    for d in range(1, n_bus):
        flow = flow + outbus_got[d - 1]
    out_all[l] = flow
    oa_copies = []
    for d in range(1, n_line):
        peer = lax.rem(l + d, n_line)
        copy = remote(
            out_all.at[l], out_all.at[l], oa_send.at[d - 1], oa_recv.at[d - 1], "line", peer
        )
        copy.start()
        oa_copies.append(copy)
    direct_t[...] = jnp.zeros_like(direct_t)
    for copy in oa_copies:
        copy.wait()
    flows = jnp.concatenate([out_all[j] for j in range(n_line)], axis=1)
    outflow_ref[...] = flows
    flow2[...] = jnp.broadcast_to((2.0 * flows)[:, None, :], flow2.shape)

    lane = lax.broadcasted_iota(jnp.int32, (8, LANES), 1)
    group = 8
    k_tiles = count_k // LANES

    def one_scenario(s, carry):
        mine = lane == s
        flow_rows = [
            flow2[s, :, t * LANES : (t + 1) * LANES] for t in range(k_tiles)
        ]

        def some_lines(g, sums):
            sums = list(sums)
            for i in range(group):
                start = pl.multiple_of((g * group + i) * 8, 8)
                here = pl.ds(start, 8)
                column = jnp.sum(jnp.where(mine, base_t[here, :], 0.0), axis=1, keepdims=True)
                limit = limit_wide[here, :]
                low = column - limit
                high = column + limit
                along = jnp.zeros((8, LANES), jnp.float32)
                for t in range(k_tiles):
                    factor = lodf_ref[here, t * LANES : (t + 1) * LANES]
                    change = factor * flow_rows[t]
                    slope = jnp.tanh(change + low) + jnp.tanh(change + high)
                    along = along + slope
                    sums[t] = sums[t] + factor * slope
                direct = jnp.sum(along, axis=1, keepdims=True)
                direct_t[here, :] = jnp.where(mine, direct, direct_t[here, :])
            return tuple(sums)

        sums = lax.fori_loop(
            0,
            count_m // (8 * group),
            some_lines,
            tuple(jnp.zeros((8, LANES), jnp.float32) for _ in range(k_tiles)),
        )
        for t in range(k_tiles):
            sens_tall[s, :, t * LANES : (t + 1) * LANES] = sums[t]
        return carry

    lax.fori_loop(0, own, one_scenario, 0)
    sens_part[...] = 0.5 * jnp.sum(sens_tall[...], axis=1)
    sens_got[l] = sens_part[...]
    se_copies = []
    for d in range(1, n_line):
        peer = lax.rem(l + d, n_line)
        copy = remote(
            sens_part, sens_got.at[l], se_send.at[d - 1], se_recv.at[d - 1], "line", peer
        )
        copy.start()
        se_copies.append(copy)
    direct = direct_t[...].T[:own, :] * (0.5 / count_k)
    match = (monitored_ref[...] == outages_ref[...]).astype(jnp.float32)
    for copy in se_copies:
        copy.wait()
    total = sens_got[0]
    for j in range(1, n_line):
        total = total + sens_got[j]
    sens_ref[...] = total * (1.0 / math.sqrt(count_m * n_line))
    backward = total * (1.0 / count_k)
    direct = direct + lax.dot_general(
        backward, match, ROWS_DOT, precision=HIGH, preferred_element_type=jnp.float32
    )
    adjoint[own_rows, :count_m] = direct.astype(jnp.bfloat16)
    adjoint[own_rows, count_m:] = (backward * keep_ref[...]).astype(jnp.bfloat16)
    ad_copies = []
    for d in range(1, n_bus):
        peer = lax.rem(b + d, n_bus)
        copy = remote(
            adjoint.at[own_rows, :],
            adjoint.at[own_rows, :],
            ad_send.at[d - 1],
            ad_recv.at[d - 1],
            "bus",
            peer,
        )
        copy.start()
        ad_copies.append(copy)
    for copy in ad_copies:
        copy.wait()

    core = lax.rem(l, 2)
    hi = l // 2
    pair = l + 1 - 2 * core
    core_copies = []
    for h in range(n_hi):
        rows = pl.ds(pl.multiple_of((2 * h + 1 - core) * grad_rows, grad_rows), grad_rows)
        core_part[h] = jnp.dot(adjoint[rows, :], rows_ref[...], preferred_element_type=jnp.float32)
        copy = remote(core_part.at[h], core_got.at[h], co_send.at[h], co_recv.at[h], "line", pair)
        copy.start()
        core_copies.append(copy)
    for h in range(n_hi):
        rows = pl.ds(pl.multiple_of((2 * h + core) * grad_rows, grad_rows), grad_rows)
        own_part[h] = jnp.dot(adjoint[rows, :], rows_ref[...], preferred_element_type=jnp.float32)
    for copy in core_copies:
        copy.wait()
    hi_copies = []
    for d in range(1, n_hi):
        other = lax.rem(hi + d, n_hi)
        hi_send[d - 1] = (own_part[other] + core_got[other]).astype(jnp.bfloat16)
        copy = remote(
            hi_send.at[d - 1],
            hi_got.at[d - 1],
            hi_ssem.at[d - 1],
            hi_rsem.at[d - 1],
            "line",
            2 * other + core,
        )
        copy.start()
        hi_copies.append(copy)
    mine = pl.ds(pl.multiple_of(l * grad_rows, grad_rows), grad_rows)
    total = own_part[hi] + core_got[hi]
    total = total + cost_ref[...] * generation_ref[mine, :].astype(jnp.float32)
    for copy in hi_copies:
        copy.wait()
    for d in range(1, n_hi):
        total = total + hi_got[d - 1].astype(jnp.float32)
    gradient_ref[...] = total.astype(jnp.bfloat16)


def on_device(
    n_bus, n_line, generation, profiles, scen_profile, ptdf, lodf, limits, monitored, outages, cost_quad
):
    profile_count = profiles.shape[0]
    profile_pick = (
        scen_profile[:, None] == jnp.arange(profile_count, dtype=jnp.int32)[None, :]
    ).astype(jnp.float32)
    loads = jnp.dot(profile_pick, profiles, precision=HIGH)
    injection = (generation.astype(jnp.float32) - loads).astype(jnp.bfloat16)
    line_rows = ptdf.shape[0]
    scen, buses = injection.shape
    count_m, count_k = lodf.shape
    first_line = lax.axis_index("line") * line_rows
    local_outages = outages - first_line
    local_monitored = monitored - first_line
    positions = jnp.arange(line_rows, dtype=jnp.int32)
    picker = (local_outages[:, None] == positions[None, :]).astype(jnp.bfloat16)
    watched_rows = jnp.take(ptdf, local_monitored, axis=0, mode="clip")
    outage_rows = jnp.dot(picker, ptdf, preferred_element_type=jnp.float32).astype(jnp.bfloat16)
    used_rows = jnp.concatenate([watched_rows, outage_rows], axis=0)
    seen = jnp.any(monitored[:, None] == outages[None, :], axis=0)
    keep = (local_outages >= 0) & (local_outages < line_rows) & jnp.logical_not(seen)
    keep = keep.astype(jnp.float32)[None, :]

    own = scen // n_bus
    width = count_k // n_line
    grad_rows = scen // n_line
    n_hi = n_line // 2
    vmem = pl.BlockSpec(memory_space=pltpu.VMEM)
    f32 = jnp.float32
    bf16 = jnp.bfloat16
    dma = pltpu.SemaphoreType.DMA
    return pl.pallas_call(
        functools.partial(step_kernel, n_bus, n_line),
        out_shape=(
            jax.ShapeDtypeStruct((grad_rows, buses), bf16),
            jax.ShapeDtypeStruct((own, count_k), f32),
            jax.ShapeDtypeStruct((own, count_k), f32),
        ),
        in_specs=[vmem] * 9,
        out_specs=(vmem, vmem, vmem),
        scratch_shapes=[
            pltpu.VMEM((n_line, scen, width), f32),
            pltpu.VMEM((n_line - 1, scen, width), f32),
            pltpu.VMEM((scen, width), f32),
            pltpu.VMEM((scen, count_m), f32),
            pltpu.VMEM((n_bus - 1, own, count_m), f32),
            pltpu.VMEM((n_bus - 1, own, width), f32),
            pltpu.VMEM((n_line, own, width), f32),
            pltpu.VMEM((count_m, LANES), f32),
            pltpu.VMEM((count_m, LANES), f32),
            pltpu.VMEM((count_m, LANES), f32),
            pltpu.VMEM((own, 8, count_k), f32),
            pltpu.VMEM((own, 8, count_k), f32),
            pltpu.VMEM((own, count_k), f32),
            pltpu.VMEM((n_line, own, count_k), f32),
            pltpu.VMEM((scen, count_m + count_k), bf16),
            pltpu.VMEM((n_hi, grad_rows, buses), f32),
            pltpu.VMEM((n_hi, grad_rows, buses), f32),
            pltpu.VMEM((n_hi, grad_rows, buses), f32),
            pltpu.VMEM((n_hi - 1, grad_rows, buses), bf16),
            pltpu.VMEM((n_hi - 1, grad_rows, buses), bf16),
            dma((n_line - 1,)),
            dma((n_line - 1,)),
            dma((n_bus - 1,)),
            dma((n_bus - 1,)),
            dma((n_bus - 1,)),
            dma((n_bus - 1,)),
            dma((n_line - 1,)),
            dma((n_line - 1,)),
            dma((n_line - 1,)),
            dma((n_line - 1,)),
            dma((n_bus - 1,)),
            dma((n_bus - 1,)),
            dma((n_hi,)),
            dma((n_hi,)),
            dma((n_hi - 1,)),
            dma((n_hi - 1,)),
        ],
        compiler_params=pltpu.CompilerParams(
            collective_id=0, has_side_effects=True, vmem_limit_bytes=56 * 1024 * 1024
        ),
    )(
        injection,
        used_rows,
        lodf,
        limits[:, None],
        monitored[:, None],
        outages[None, :],
        keep,
        generation,
        cost_quad[None, :],
    )


def solution(mesh):
    placed = (
        P(None, "bus"),
        P(None, "bus"),
        P(),
        P("line", "bus"),
        P("line", None),
        P("line"),
        P("line"),
        P(),
        P("bus"),
    )
    return jax.shard_map(
        functools.partial(on_device, mesh.shape["bus"], mesh.shape["line"]),
        mesh=mesh,
        in_specs=placed,
        out_specs=(P("line", "bus"), P("bus", None), P("bus", None)),
        check_vma=False,
    )
```

```python
import functools
import math

import jax
import jax.numpy as jnp
from jax import lax
from jax.experimental import pallas as pl
from jax.experimental.pallas import tpu as pltpu
from jax.sharding import PartitionSpec as P

MESH = pl.DeviceIdType.MESH
HIGH = lax.Precision.HIGHEST
ROWS_DOT = (((1,), (1,)), ((), ()))
LANES = 128


def remote(src, dst, send_sem, recv_sem, axis, peer):
    return pltpu.make_async_remote_copy(
        src_ref=src,
        dst_ref=dst,
        send_sem=send_sem,
        recv_sem=recv_sem,
        device_id={axis: peer},
        device_id_type=MESH,
    )


def step_kernel(
    n_bus,
    n_line,
    inj_ref,
    rows_ref,
    lodf_ref,
    limits_ref,
    monitored_ref,
    outages_ref,
    keep_ref,
    generation_ref,
    cost_ref,
    gradient_ref,
    outflow_ref,
    sens_ref,
    out_part,
    out_got,
    out_sum,
    mon_part,
    mon_got,
    outbus_got,
    out_all,
    base_parts,
    limit_wide,
    wide,
    direct_tall,
    flow2,
    sens_tall,
    sens_part,
    sens_got,
    adjoint,
    core_part,
    core_got,
    own_part,
    hi_send,
    hi_got,
    line_send,
    line_recv,
    mon_send,
    mon_recv,
    ob_send,
    ob_recv,
    oa_send,
    oa_recv,
    se_send,
    se_recv,
    ad_send,
    ad_recv,
    co_send,
    co_recv,
    hi_ssem,
    hi_rsem,
):
    scen, buses = inj_ref.shape
    count_m, count_k = lodf_ref.shape
    own = scen // n_bus
    width = count_k // n_line
    grad_rows = scen // n_line
    n_hi = n_line // 2
    b = lax.axis_index("bus")
    l = lax.axis_index("line")

    barrier = pltpu.get_barrier_semaphore()
    for d in range(1, n_bus):
        pl.semaphore_signal(
            barrier, inc=1, device_id={"bus": lax.rem(b + d, n_bus)}, device_id_type=MESH
        )
    for d in range(1, n_line):
        pl.semaphore_signal(
            barrier, inc=1, device_id={"line": lax.rem(l + d, n_line)}, device_id_type=MESH
        )
    for j in range(n_line):
        out_part[j] = lax.dot_general(
            inj_ref[...],
            rows_ref[count_m + j * width : count_m + (j + 1) * width, :],
            ROWS_DOT,
            preferred_element_type=jnp.float32,
        )
    pl.semaphore_wait(barrier, n_bus + n_line - 2)
    line_copies = []
    for d in range(1, n_line):
        peer = lax.rem(l + d, n_line)
        copy = remote(
            out_part.at[peer], out_got.at[d - 1], line_send.at[d - 1], line_recv.at[d - 1], "line", peer
        )
        copy.start()
        line_copies.append(copy)
    mon_part[...] = lax.dot_general(
        inj_ref[...], rows_ref[:count_m, :], ROWS_DOT, preferred_element_type=jnp.float32
    )
    mon_copies = []
    for d in range(1, n_bus):
        peer = lax.rem(b + d, n_bus)
        copy = remote(
            mon_part.at[pl.ds(pl.multiple_of(peer * own, own), own), :],
            mon_got.at[d - 1],
            mon_send.at[d - 1],
            mon_recv.at[d - 1],
            "bus",
            peer,
        )
        copy.start()
        mon_copies.append(copy)
    limit_wide[...] = jnp.broadcast_to(2.0 * limits_ref[...], limit_wide.shape)
    for copy in line_copies:
        copy.wait()
    total = out_part[l]
    for d in range(1, n_line):
        total = total + out_got[d - 1]
    out_sum[...] = total
    ob_copies = []
    for d in range(1, n_bus):
        peer = lax.rem(b + d, n_bus)
        copy = remote(
            out_sum.at[pl.ds(pl.multiple_of(peer * own, own), own), :],
            outbus_got.at[d - 1],
            ob_send.at[d - 1],
            ob_recv.at[d - 1],
            "bus",
            peer,
        )
        copy.start()
        ob_copies.append(copy)
    own_rows = pl.ds(pl.multiple_of(b * own, own), own)
    for copy in mon_copies:
        copy.wait()
    base = mon_part[own_rows, :]
    for d in range(1, n_bus):
        base = base + mon_got[d - 1]
    spread = jnp.concatenate([2.0 * base, jnp.zeros((LANES - own, count_m), jnp.float32)], axis=0)
    turned = spread.T
    head = turned.astype(jnp.bfloat16)
    rest = turned - head.astype(jnp.float32)
    middle = rest.astype(jnp.bfloat16)
    tail = (rest - middle.astype(jnp.float32)).astype(jnp.bfloat16)
    base_parts[...] = jnp.concatenate([head, middle, tail], axis=1)

    def widen(s, carry):
        row = lax.broadcasted_iota(jnp.int32, (3 * LANES, LANES), 0)
        chosen = (row == s) | (row == s + LANES) | (row == s + 2 * LANES)
        selector = jnp.where(chosen, 1.0, 0.0).astype(jnp.bfloat16)
        wide[s] = jnp.dot(base_parts[...], selector, preferred_element_type=jnp.float32)
        return carry

    lax.fori_loop(0, own, widen, 0, unroll=2)
    for copy in ob_copies:
        copy.wait()
    flow = out_sum[own_rows, :]
    for d in range(1, n_bus):
        flow = flow + outbus_got[d - 1]
    out_all[l] = flow
    oa_copies = []
    for d in range(1, n_line):
        peer = lax.rem(l + d, n_line)
        copy = remote(
            out_all.at[l], out_all.at[l], oa_send.at[d - 1], oa_recv.at[d - 1], "line", peer
        )
        copy.start()
        oa_copies.append(copy)
    for copy in oa_copies:
        copy.wait()
    flows = jnp.concatenate([out_all[j] for j in range(n_line)], axis=1)
    outflow_ref[...] = flows
    flow2[...] = jnp.broadcast_to((2.0 * flows)[:, None, :], flow2.shape)

    group = 8
    k_tiles = count_k // LANES

    def one_scenario(s, carry):
        flow_rows = [
            flow2[s, :, t * LANES : (t + 1) * LANES] for t in range(k_tiles)
        ]

        def some_lines(g, sums):
            sums = list(sums)
            for i in range(group):
                start = pl.multiple_of((g * group + i) * 8, 8)
                here = pl.ds(start, 8)
                column = wide[s, here, :]
                limit = limit_wide[here, :]
                low = column - limit
                high = column + limit
                along = jnp.zeros((8, LANES), jnp.float32)
                for t in range(k_tiles):
                    factor = lodf_ref[here, t * LANES : (t + 1) * LANES]
                    change = factor * flow_rows[t]
                    slope = jnp.tanh(change + low) + jnp.tanh(change + high)
                    along = along + slope
                    sums[t] = sums[t] + factor * slope
                wide[s, here, :] = along
            return tuple(sums)

        sums = lax.fori_loop(
            0,
            count_m // (8 * group),
            some_lines,
            tuple(jnp.zeros((8, LANES), jnp.float32) for _ in range(k_tiles)),
        )
        for t in range(k_tiles):
            sens_tall[s, :, t * LANES : (t + 1) * LANES] = sums[t]
        return carry

    lax.fori_loop(0, own, one_scenario, 0)
    sens_part[...] = 0.5 * jnp.sum(sens_tall[...], axis=1)
    sens_got[l] = sens_part[...]
    se_copies = []
    for d in range(1, n_line):
        peer = lax.rem(l + d, n_line)
        copy = remote(
            sens_part, sens_got.at[l], se_send.at[d - 1], se_recv.at[d - 1], "line", peer
        )
        copy.start()
        se_copies.append(copy)
    ones = jnp.ones((16, 2 * LANES), jnp.bfloat16)

    def add_lanes(s, carry):
        along = wide[s]
        head = along.astype(jnp.bfloat16)
        rest = (along - head.astype(jnp.float32)).astype(jnp.bfloat16)
        both = jnp.concatenate([head, rest], axis=1)
        sums = lax.dot_general(ones, both, ROWS_DOT, preferred_element_type=jnp.float32)
        direct_tall[s] = sums[:8, :]
        return carry

    lax.fori_loop(0, own, add_lanes, 0, unroll=2)
    direct = jnp.sum(direct_tall[...], axis=1) * (0.0625 / count_k)
    match = (monitored_ref[...] == outages_ref[...]).astype(jnp.float32)
    for copy in se_copies:
        copy.wait()
    total = sens_got[0]
    for j in range(1, n_line):
        total = total + sens_got[j]
    sens_ref[...] = total * (1.0 / math.sqrt(count_m * n_line))
    backward = total * (1.0 / count_k)
    direct = direct + lax.dot_general(
        backward, match, ROWS_DOT, precision=HIGH, preferred_element_type=jnp.float32
    )
    adjoint[own_rows, :count_m] = direct.astype(jnp.bfloat16)
    adjoint[own_rows, count_m:] = (backward * keep_ref[...]).astype(jnp.bfloat16)
    ad_copies = []
    for d in range(1, n_bus):
        peer = lax.rem(b + d, n_bus)
        copy = remote(
            adjoint.at[own_rows, :],
            adjoint.at[own_rows, :],
            ad_send.at[d - 1],
            ad_recv.at[d - 1],
            "bus",
            peer,
        )
        copy.start()
        ad_copies.append(copy)
    for copy in ad_copies:
        copy.wait()

    core = lax.rem(l, 2)
    hi = l // 2
    pair = l + 1 - 2 * core
    core_copies = []
    for h in range(n_hi):
        rows = pl.ds(pl.multiple_of((2 * h + 1 - core) * grad_rows, grad_rows), grad_rows)
        core_part[h] = jnp.dot(adjoint[rows, :], rows_ref[...], preferred_element_type=jnp.float32)
        copy = remote(core_part.at[h], core_got.at[h], co_send.at[h], co_recv.at[h], "line", pair)
        copy.start()
        core_copies.append(copy)
    for h in range(n_hi):
        rows = pl.ds(pl.multiple_of((2 * h + core) * grad_rows, grad_rows), grad_rows)
        own_part[h] = jnp.dot(adjoint[rows, :], rows_ref[...], preferred_element_type=jnp.float32)
    for copy in core_copies:
        copy.wait()
    hi_copies = []
    for d in range(1, n_hi):
        other = lax.rem(hi + d, n_hi)
        hi_send[d - 1] = (own_part[other] + core_got[other]).astype(jnp.bfloat16)
        copy = remote(
            hi_send.at[d - 1],
            hi_got.at[d - 1],
            hi_ssem.at[d - 1],
            hi_rsem.at[d - 1],
            "line",
            2 * other + core,
        )
        copy.start()
        hi_copies.append(copy)
    mine = pl.ds(pl.multiple_of(l * grad_rows, grad_rows), grad_rows)
    total = own_part[hi] + core_got[hi]
    total = total + cost_ref[...] * generation_ref[mine, :].astype(jnp.float32)
    for copy in hi_copies:
        copy.wait()
    for d in range(1, n_hi):
        total = total + hi_got[d - 1].astype(jnp.float32)
    gradient_ref[...] = total.astype(jnp.bfloat16)


def pick_kernel(ids_ref, ptdf_ref, rows_ref, picker):
    used, lines = picker.shape

    @pl.when(pl.program_id(0) == 0)
    def _():
        ids = ids_ref[...]
        for start in range(0, lines, 512):
            place = start + lax.broadcasted_iota(jnp.int32, (used, 512), 1)
            picker[:, start : start + 512] = jnp.where(ids == place, 1.0, 0.0).astype(jnp.bfloat16)

    rows_ref[...] = jnp.dot(
        picker[...], ptdf_ref[...], preferred_element_type=jnp.float32
    ).astype(jnp.bfloat16)


def pick_rows(ids, ptdf):
    lines, buses = ptdf.shape
    used = ids.shape[0]
    block = 256
    return pl.pallas_call(
        pick_kernel,
        grid=(buses // block,),
        out_shape=jax.ShapeDtypeStruct((used, buses), jnp.bfloat16),
        in_specs=[
            pl.BlockSpec((used, 1), lambda i: (0, 0)),
            pl.BlockSpec((lines, block), lambda i: (0, i)),
        ],
        out_specs=pl.BlockSpec((used, block), lambda i: (0, i)),
        scratch_shapes=[pltpu.VMEM((used, lines), jnp.bfloat16)],
        compiler_params=pltpu.CompilerParams(vmem_limit_bytes=48 * 1024 * 1024),
    )(ids[:, None], ptdf)


def on_device(
    n_bus, n_line, generation, profiles, scen_profile, ptdf, lodf, limits, monitored, outages, cost_quad
):
    profile_count = profiles.shape[0]
    profile_pick = (
        scen_profile[:, None] == jnp.arange(profile_count, dtype=jnp.int32)[None, :]
    ).astype(jnp.float32)
    loads = jnp.dot(profile_pick, profiles, precision=HIGH)
    injection = (generation.astype(jnp.float32) - loads).astype(jnp.bfloat16)
    line_rows = ptdf.shape[0]
    scen, buses = injection.shape
    count_m, count_k = lodf.shape
    first_line = lax.axis_index("line") * line_rows
    local_outages = outages - first_line
    local_used = jnp.concatenate([monitored - first_line, local_outages])
    used_rows = pick_rows(local_used, ptdf)
    seen = jnp.any(monitored[:, None] == outages[None, :], axis=0)
    keep = (local_outages >= 0) & (local_outages < line_rows) & jnp.logical_not(seen)
    keep = keep.astype(jnp.float32)[None, :]

    own = scen // n_bus
    width = count_k // n_line
    grad_rows = scen // n_line
    n_hi = n_line // 2
    vmem = pl.BlockSpec(memory_space=pltpu.VMEM)
    f32 = jnp.float32
    bf16 = jnp.bfloat16
    dma = pltpu.SemaphoreType.DMA
    return pl.pallas_call(
        functools.partial(step_kernel, n_bus, n_line),
        out_shape=(
            jax.ShapeDtypeStruct((grad_rows, buses), bf16),
            jax.ShapeDtypeStruct((own, count_k), f32),
            jax.ShapeDtypeStruct((own, count_k), f32),
        ),
        in_specs=[vmem] * 9,
        out_specs=(vmem, vmem, vmem),
        scratch_shapes=[
            pltpu.VMEM((n_line, scen, width), f32),
            pltpu.VMEM((n_line - 1, scen, width), f32),
            pltpu.VMEM((scen, width), f32),
            pltpu.VMEM((scen, count_m), f32),
            pltpu.VMEM((n_bus - 1, own, count_m), f32),
            pltpu.VMEM((n_bus - 1, own, width), f32),
            pltpu.VMEM((n_line, own, width), f32),
            pltpu.VMEM((count_m, 3 * LANES), bf16),
            pltpu.VMEM((count_m, LANES), f32),
            pltpu.VMEM((own, count_m, LANES), f32),
            pltpu.VMEM((own, 8, count_m), f32),
            pltpu.VMEM((own, 8, count_k), f32),
            pltpu.VMEM((own, 8, count_k), f32),
            pltpu.VMEM((own, count_k), f32),
            pltpu.VMEM((n_line, own, count_k), f32),
            pltpu.VMEM((scen, count_m + count_k), bf16),
            pltpu.VMEM((n_hi, grad_rows, buses), f32),
            pltpu.VMEM((n_hi, grad_rows, buses), f32),
            pltpu.VMEM((n_hi, grad_rows, buses), f32),
            pltpu.VMEM((n_hi - 1, grad_rows, buses), bf16),
            pltpu.VMEM((n_hi - 1, grad_rows, buses), bf16),
            dma((n_line - 1,)),
            dma((n_line - 1,)),
            dma((n_bus - 1,)),
            dma((n_bus - 1,)),
            dma((n_bus - 1,)),
            dma((n_bus - 1,)),
            dma((n_line - 1,)),
            dma((n_line - 1,)),
            dma((n_line - 1,)),
            dma((n_line - 1,)),
            dma((n_bus - 1,)),
            dma((n_bus - 1,)),
            dma((n_hi,)),
            dma((n_hi,)),
            dma((n_hi - 1,)),
            dma((n_hi - 1,)),
        ],
        compiler_params=pltpu.CompilerParams(
            collective_id=0, has_side_effects=True, vmem_limit_bytes=58 * 1024 * 1024
        ),
    )(
        injection,
        used_rows,
        lodf,
        limits[:, None],
        monitored[:, None],
        outages[None, :],
        keep,
        generation,
        cost_quad[None, :],
    )


def solution(mesh):
    placed = (
        P(None, "bus"),
        P(None, "bus"),
        P(),
        P("line", "bus"),
        P("line", None),
        P("line"),
        P("line"),
        P(),
        P("bus"),
    )
    return jax.shard_map(
        functools.partial(on_device, mesh.shape["bus"], mesh.shape["line"]),
        mesh=mesh,
        in_specs=placed,
        out_specs=(P("line", "bus"), P("bus", None), P("bus", None)),
        check_vma=False,
    )
```
